32 devices in a mesh: box: 8 (over y, x, core), group: 4 (over z).
Axes of the slice: x: 2, y: 2, z: 4, core: 2. Of those that a mesh axis runs over, the one named last changes fastest.
Arguments:
- right_side: float32 [128, 128, 512], P('box', 'group'), may hold values from -6 to 6
- inv_density: float32 [128, 128, 512], P('box', 'group'), may hold values from 0.2 to 5
- pressure: float32 [128, 128, 512], P('box', 'group'), may hold values from -6 to 6
Outputs:
- corrected: float32 [128, 128, 512], P('box', 'group')
The draws below stay inside these ranges and needn't reach their ends.
All inputs are finite; a program needn't handle non-finite values.
Results may differ from the reference program's by a relative error of at most 0.0003.
Values sent between devices are 32-bit elements; how exact they have to be, the bound alone decides.
A program may use at most 128 MiB of HBM per device.

```python
import math
import jax
import jax.numpy as jnp

CZ = 512
SWEEPS = 2
CHEB = 8
NX = 128
NY = 128


def block_scale(rng, extent, shards, low, high):
    gain, own = 1.0, jax.random.fold_in(rng, 6)
    for position, blocks in shards:
        steps = jnp.exp(jax.random.uniform(jax.random.fold_in(own, position), (blocks,), jnp.float32, low / len(shards), high / len(shards)))
        gain = gain * jnp.repeat(steps, extent[position] // blocks).reshape([-1 if axis == position else 1 for axis in range(len(extent))])
    return gain


def bell_draw(own_key, dims, scale, reach, pieces=(), held_as=jnp.bfloat16):
    factor_of = block_scale(own_key, dims, pieces, -0.22, 0.18) if pieces else 1.0
    drawn = jax.random.normal(own_key, dims, jnp.float32) * scale * factor_of
    return jnp.minimum(jnp.maximum(drawn, -reach), reach).astype(held_as)


def setup_inputs(seed: int = 0) -> dict:
    splits = jax.random.split(jax.random.key(seed), 4)
    right_side = bell_draw(splits[0], (NX, NY, CZ), 1.0, 6.0, ((0, 8), (1, 4)), jnp.float32)
    inv_density = jnp.clip(jnp.exp(math.log(5.0) - 3.218876 * jax.random.uniform(splits[1], (NX, NY, CZ), jnp.float32) ** block_scale(splits[1], (NX, NY, CZ), ((0, 8), (1, 4)), -0.2, 0.2)), 0.2, 5.0)
    pressure = bell_draw(splits[2], (NX, NY, CZ), 1.0, 6.0, ((0, 8), (1, 4)), jnp.float32)
    return {"right_side": right_side, "inv_density": inv_density, "pressure": pressure}


def neighbours(padded):
    return [padded[:-2, 1:-1, 1:-1], padded[2:, 1:-1, 1:-1],
            padded[1:-1, :-2, 1:-1], padded[1:-1, 2:, 1:-1],
            padded[1:-1, 1:-1, :-2], padded[1:-1, 1:-1, 2:]]


def face_coefs(field, padded):
    return [jnp.where(near > 0, 2.0 * field * near / (field + near), field) for near in neighbours(padded)]


def stencil(field, padded, coefs):
    total = jnp.zeros_like(field)
    for coef, near in zip(coefs, neighbours(padded)):
        total = total + coef * (field - near)
    return total


def block_mean(field):
    sx, sy, sz = field.shape
    return field.reshape(sx // 4, 4, sy // 4, 4, sz // 4, 4).mean(axis=(1, 3, 5))


def chebyshev(rhs_c, coefs, diag, padder):
    low, high = 0.05, 2.0
    theta = (high + low) / 2.0
    delta = (high - low) / 2.0
    sigma = theta / delta
    rho = 1.0 / sigma
    solution = jnp.zeros_like(rhs_c)
    remain = rhs_c
    direction = remain / (diag * theta)
    for step in range(CHEB):
        solution = solution + direction
        if step + 1 < CHEB:
            remain = remain - stencil(direction, padder(direction), coefs)
            rho_next = 1.0 / (2.0 * sigma - rho)
            direction = rho_next * rho * direction + (2.0 * rho_next / delta) * remain / diag
            rho = rho_next
    return solution


def zero_pad(field):
    return jnp.pad(field, 1)


def reference(right_side, inv_density, pressure):
    coefs = face_coefs(inv_density, zero_pad(inv_density))
    diag = sum(coefs)
    fine = pressure
    for sweep in range(SWEEPS):
        fine = fine + (2.0 / 3.0) * (right_side - stencil(fine, zero_pad(fine), coefs)) / diag
    res = right_side - stencil(fine, zero_pad(fine), coefs)
    coarse_rhs = block_mean(res)
    coarse_b = block_mean(inv_density)
    coarse_coefs = [c * 0.0625 for c in face_coefs(coarse_b, zero_pad(coarse_b))]
    coarse_diag = sum(coarse_coefs)
    corr = chebyshev(coarse_rhs, coarse_coefs, coarse_diag, zero_pad)
    expanded = jnp.repeat(jnp.repeat(jnp.repeat(corr, 4, axis=0), 4, axis=1), 4, axis=2)
    return fine + expanded
```

```python
import functools

import jax
import jax.numpy as jnp
from jax import lax
from jax.experimental import pallas as pl
from jax.experimental.pallas import tpu as pltpu
from jax.sharding import PartitionSpec as P

CHEB = 8
POOL = 4
MESH = pl.DeviceIdType.MESH


def chebyshev_factors():
    low, high = 0.05, 2.0
    theta = (high + low) / 2.0
    delta = (high - low) / 2.0
    sigma = theta / delta
    rho = 1.0 / sigma
    steps = []
    for _ in range(CHEB - 1):
        rho_next = 1.0 / (2.0 * sigma - rho)
        steps.append((rho_next * rho, 2.0 * rho_next / delta))
        rho = rho_next
    return 1.0 / theta, steps


def inverse(x):
    r = pl.reciprocal(x, approx=True)
    return r * (2.0 - x * r)


def face(a, b):
    m = a * b
    return (m + m) * inverse(a + b)


def edge_face(a, b):
    m = a * b
    s = a + b
    return jnp.where(m > 0, (m + m) * inverse(s), s)


def split(x):
    hi = x.astype(jnp.bfloat16)
    return hi, (x - hi.astype(jnp.float32)).astype(jnp.bfloat16)


def dot(a, b):
    return jnp.dot(a, b, preferred_element_type=jnp.float32)


def members(rows, cols, long_first):
    r = lax.broadcasted_iota(jnp.int32, (rows, cols), 0)
    c = lax.broadcasted_iota(jnp.int32, (rows, cols), 1)
    same = (r // POOL == c) if long_first else (r == c // POOL)
    return same.astype(jnp.float32).astype(jnp.bfloat16)


def pool(stack):
    g, rows, lanes = stack.shape
    flat = stack.reshape(g * rows, lanes)
    across = members(lanes, lanes // POOL, True)
    hi, lo = split(flat)
    m = dot(hi, across) + dot(lo, across)
    down = members(g * rows // POOL, g * rows, False)
    hi, lo = split(m)
    return (dot(down, hi) + dot(down, lo)) * (1.0 / POOL**3)


def cycle_kernel(
    nb, ng, f_hbm, b_hbm, p_hbm, fine_hbm, e_ref,
    V0, B, V1, V2, F, CX, CY, CZ, W, D, T, ysend, yrecv, yface, ygain,
    ACC, GB, GR, KX, KY, KZ, KW, DD,
    lsem, fsend, frecv, csend, crecv,
):
    nx, ny, nz = F.shape
    cx, cy, cz = nx // POOL, ny // POOL, nz // POOL
    hb, hg = (GB.shape[0] // cx - 1) // 2, (GB.shape[1] // cy - 1) // 2
    bx, gx = lax.axis_index("box"), lax.axis_index("group")

    def there(dx, dg):
        ok = (bx + dx >= 0) & (bx + dx < nb)
        return ok & (gx + dg >= 0) & (gx + dg < ng)

    offsets = [
        (dx, dg)
        for dg in range(-hg, hg + 1)
        for dx in range(-hb, hb + 1)
        if (dx, dg) != (0, 0)
    ]
    barrier = pltpu.get_barrier_semaphore()
    for dx, dg in offsets:
        @pl.when(there(dx, dg))
        def _():
            pl.semaphore_signal(
                barrier, inc=1, device_id={"box": bx + dx, "group": gx + dg}, device_id_type=MESH
            )

    inside = pl.ds(1, nx)
    load_b = pltpu.make_async_copy(b_hbm, B.at[inside], lsem.at[0])
    load_p = pltpu.make_async_copy(p_hbm, V0.at[inside], lsem.at[1])
    load_f = pltpu.make_async_copy(f_hbm, F, lsem.at[2])
    load_b.start()
    load_p.start()
    load_f.start()

    fields = [V0, B, V1, V2]
    goes = [(1, 0), (-1, 0), (0, 1), (0, -1)]

    def fine_copy(a, way):
        if way == 0:
            src = (p_hbm, b_hbm)[a].at[nx - 1] if a < 2 else fields[a].at[nx]
            dst = fields[a].at[0]
        elif way == 1:
            src = (p_hbm, b_hbm)[a].at[0] if a < 2 else fields[a].at[1]
            dst = fields[a].at[nx + 1]
        else:
            src, dst = ysend.at[a, 3 - way], yrecv.at[a, way - 2]
        dx, dg = goes[way]
        return pltpu.make_async_remote_copy(
            src_ref=src, dst_ref=dst, send_sem=fsend.at[a, way], recv_sem=frecv.at[a, way],
            device_id={"box": bx + dx, "group": gx + dg}, device_id_type=MESH,
        )

    def send(a, ways):
        for way in ways:
            @pl.when(there(*goes[way]))
            def _():
                fine_copy(a, way).start()

    def receive(a, ways):
        for way in ways:
            @pl.when(there(-goes[way][0], -goes[way][1]))
            def _():
                fine_copy(a, way).wait_recv()

    def coarse_copy(a, o):
        dx, dg = offsets[o]
        G = (GB, GR)[a]
        return pltpu.make_async_remote_copy(
            src_ref=G.at[pl.ds(hb * cx, cx), pl.ds(hg * cy, cy)],
            dst_ref=G.at[pl.ds((hb - dx) * cx, cx), pl.ds((hg - dg) * cy, cy)],
            send_sem=csend.at[a, o], recv_sem=crecv.at[a, o],
            device_id={"box": bx + dx, "group": gx + dg}, device_id_type=MESH,
        )

    def coarse_send(a):
        for o, (dx, dg) in enumerate(offsets):
            @pl.when(there(dx, dg))
            def _():
                coarse_copy(a, o).start()

    def coarse_receive(a):
        for o, (dx, dg) in enumerate(offsets):
            @pl.when(there(-dx, -dg))
            def _():
                coarse_copy(a, o).wait_recv()

    for way in (0, 1):
        @pl.when(jnp.logical_not(there(-goes[way][0], 0)))
        def _():
            for field in fields:
                field[way * (nx + 1)] = jnp.zeros((ny, nz), jnp.float32)
    for way in (2, 3):
        @pl.when(jnp.logical_not(there(0, -goes[way][1])))
        def _():
            for a in range(4):
                yrecv[a, way - 2] = jnp.zeros((nx, nz), jnp.float32)
    for dx, dg in offsets:
        @pl.when(jnp.logical_not(there(dx, dg)))
        def _():
            for G in (GB, GR):
                G[pl.ds((hb + dx) * cx, cx), pl.ds((hg + dg) * cy, cy)] = jnp.zeros(
                    (cx, cy, cz), jnp.float32
                )

    neighbours = 0
    for dx, dg in offsets:
        neighbours = neighbours + there(dx, dg).astype(jnp.int32)
    pl.semaphore_wait(barrier, neighbours)
    send(1, (0, 1))
    send(0, (0, 1))

    def pack(a):
        ysend[a, 0] = fields[a][pl.ds(1, nx), 0, :]
        ysend[a, 1] = fields[a][pl.ds(1, nx), ny - 1, :]

    load_b.wait()
    pack(1)
    send(1, (2, 3))
    load_p.wait()
    pack(0)
    send(0, (2, 3))
    load_f.wait()

    lane = lax.broadcasted_iota(jnp.int32, (ny, nz), 1)
    row = lax.broadcasted_iota(jnp.int32, (ny, nz), 0)
    low_row = lax.broadcasted_iota(jnp.int32, (8, nz), 0) == 0
    high_row = lax.broadcasted_iota(jnp.int32, (8, nz), 0) == 7

    def in_plane(v, ky, kz):
        s = kz * pltpu.roll(v, nz - 1, 1) + pltpu.roll(kz * v, 1, 1)
        return s + (ky * pltpu.roll(v, ny - 1, 0) + pltpu.roll(ky * v, 1, 0))

    def add_rows(t, low, high):
        return jnp.concatenate(
            [
                t[0:8] + jnp.where(low_row, low, 0.0),
                t[8 : ny - 8],
                t[ny - 8 : ny] + jnp.where(high_row, high, 0.0),
            ],
            axis=0,
        )

    def before_halo(i, first=False):
        b, p = B[i + 1], V0[i + 1]
        kz = jnp.where(lane == nz - 1, 0.0, face(b, pltpu.roll(b, nz - 1, 1)))
        ky = jnp.where(row == ny - 1, 0.0, face(b, pltpu.roll(b, ny - 1, 0)))
        CZ[i] = kz
        CY[i] = ky
        if not first:
            CX[i] = face(B[i], b)
        ends = jnp.where((lane == 0) | (lane == nz - 1), b, 0.0)
        D[i] = (kz + pltpu.roll(kz, 1, 1)) + (ky + pltpu.roll(ky, 1, 0)) + ends
        T[i] = F[i] + in_plane(p, ky, kz)

    before_halo(0, True)
    lax.fori_loop(1, nx, lambda i, c: (before_halo(i), c)[1], 0)

    def sum_b(g, c):
        s = B[POOL * g + 1]
        for k in range(1, POOL):
            s = s + B[POOL * g + 1 + k]
        ACC[g] = s
        return c

    lax.fori_loop(0, cx, sum_b, 0)
    center = (pl.ds(hb * cx, cx), pl.ds(hg * cy, cy))
    GB[center] = pool(ACC[...]).reshape(cx, cy, cz)
    coarse_send(0)

    receive(1, (0, 1, 2, 3))
    CX[0] = edge_face(B[0], B[1])
    CX[nx] = edge_face(B[nx], B[nx + 1])
    for side in (0, 1):
        yface[side] = edge_face(ysend[1, side], yrecv[1, side])
    receive(0, (0, 1, 2, 3))

    def gains(a):
        for side in (0, 1):
            ygain[side] = yface[side] * yrecv[a, side]

    gains(0)

    def first_sweep(i):
        at = pl.ds(i, 1)
        k0, k1 = CX[i], CX[i + 1]
        d = add_rows(D[i] + (k0 + k1), yface[0, at, :], yface[1, at, :])
        D[i] = d
        w = (2.0 / 3.0) * inverse(d)
        W[i] = w
        t = T[i] + (k0 * V0[i] + k1 * V0[i + 2])
        t = add_rows(t, ygain[0, at, :], ygain[1, at, :])
        V1[i + 1] = (1.0 / 3.0) * V0[i + 1] + w * t

    def both_ends(step):
        lax.fori_loop(0, 2, lambda j, c: (step(j * (nx - 1)), c)[1], 0)

    def between(step):
        lax.fori_loop(1, nx - 1, lambda i, c: (step(i), c)[1], 0)

    both_ends(first_sweep)
    send(2, (0, 1))
    between(first_sweep)
    pack(2)
    send(2, (2, 3))

    def total(V, i):
        v = V[i + 1]
        x = CX[i] * V[i] + CX[i + 1] * V[i + 2]
        return v, F[i] + x + in_plane(v, CY[i], CZ[i])

    def second_sweep(i):
        v, t = total(V1, i)
        V2[i + 1] = (1.0 / 3.0) * v + W[i] * t

    between(second_sweep)
    receive(2, (0, 1))
    both_ends(second_sweep)
    receive(2, (2, 3))
    gains(2)

    bottom, top = pl.ds(0, 8), pl.ds(ny - 8, 8)

    def second_rows(i, c):
        at = pl.ds(i, 1)
        V2[i + 1, bottom, :] += jnp.where(low_row, W[i, bottom, :] * ygain[0, at, :], 0.0)
        V2[i + 1, top, :] += jnp.where(high_row, W[i, top, :] * ygain[1, at, :], 0.0)
        return c

    lax.fori_loop(0, nx, second_rows, 0)
    send(3, (0, 1))
    pack(3)
    send(3, (2, 3))
    store = pltpu.make_async_copy(V2.at[inside], fine_hbm, lsem.at[3])
    store.start()

    ACC[...] = jnp.zeros_like(ACC)

    def residual(i):
        v, t = total(V2, i)
        ACC[i // POOL] += t - D[i] * v

    between(residual)

    coarse_receive(0)
    gb = GB[...]
    ex, ey, ez = gb.shape
    clane = lax.broadcasted_iota(jnp.int32, gb.shape, 2)
    kx = edge_face(gb[:-1], gb[1:])
    ky = edge_face(gb, pltpu.roll(gb, ey - 1, 1))
    kz = jnp.where(clane == ez - 1, 0.0, edge_face(gb, pltpu.roll(gb, ez - 1, 2)))
    KX[...] = kx
    KY[...] = ky
    KZ[...] = kz
    ends = jnp.where((clane == 0) | (clane == ez - 1), gb, 0.0)
    d = (kz + pltpu.roll(kz, 1, 2)) + (ky + pltpu.roll(ky, 1, 1)) + ends
    d = d[1:-1] + (kx[:-1] + kx[1:])
    KW[pl.ds(1, ex - 2)] = jnp.where(gb[1:-1] > 0, inverse(d), 0.0)

    receive(3, (0, 1))
    both_ends(residual)
    receive(3, (2, 3))
    gains(3)

    def residual_rows(i, c):
        at, g = pl.ds(i, 1), i // POOL
        ACC[g, bottom, :] += jnp.where(low_row, ygain[0, at, :], 0.0)
        ACC[g, top, :] += jnp.where(high_row, ygain[1, at, :], 0.0)
        return c

    lax.fori_loop(0, nx, residual_rows, 0)
    GR[center] = pool(ACC[...]).reshape(cx, cy, cz)
    coarse_send(1)
    coarse_receive(1)

    start, steps = chebyshev_factors()
    lo, hi = 1, ex - 1
    q = GR[pl.ds(lo, hi - lo)] * KW[pl.ds(lo, hi - lo)] * 16.0
    d = q * start
    DD[pl.ds(lo, hi - lo)] = d
    e = DD[center]
    for decay, gain in steps:
        lo, hi = lo + 1, hi - 1
        span = pl.ds(lo, hi - lo)
        v = DD[span]
        ky, kz = KY[span], KZ[span]
        s = KX[pl.ds(lo - 1, hi - lo)] * DD[pl.ds(lo - 1, hi - lo)]
        s = s + KX[span] * DD[pl.ds(lo + 1, hi - lo)]
        s = s + (ky * pltpu.roll(v, ey - 1, 1) + pltpu.roll(ky * v, 1, 1))
        s = s + (kz * pltpu.roll(v, ez - 1, 2) + pltpu.roll(kz * v, 1, 2))
        q = q[1:-1] - v + KW[span] * s
        DD[span] = decay * v + gain * q
        e = e + DD[center]
    e_ref[...] = e.reshape(cx * cy, cz)

    for a in range(4):
        for way in range(4):
            @pl.when(there(*goes[way]))
            def _():
                fine_copy(a, way).wait_send()
    for a in range(2):
        for o, (dx, dg) in enumerate(offsets):
            @pl.when(there(dx, dg))
            def _():
                coarse_copy(a, o).wait_send()
    store.wait()


def expand_kernel(fine_ref, e_ref, out_ref):
    planes, ny, nz = fine_ref.shape
    cy, cz = e_ref.shape
    across = members(cz, nz, False)
    hi, lo = split(e_ref[...])
    wide = dot(hi, across) + dot(lo, across)
    down = members(ny, cy, True)
    hi, lo = split(wide)
    tall = dot(down, hi) + dot(down, lo)
    for k in range(planes):
        out_ref[k] = fine_ref[k] + tall


def per_device(nb, ng, right_side, inv_density, pressure):
    nx, ny, nz = right_side.shape
    cx, cy, cz = nx // POOL, ny // POOL, nz // POOL
    hb, hg = -(-CHEB // cx), -(-CHEB // cy)
    ex, ey = (2 * hb + 1) * cx, (2 * hg + 1) * cy
    count = (2 * hb + 1) * (2 * hg + 1) - 1
    f32 = jnp.float32
    block = pltpu.VMEM((nx, ny, nz), f32)
    padded = pltpu.VMEM((nx + 2, ny, nz), f32)
    coarse = pltpu.VMEM((ex, ey, cz), f32)
    dma = pltpu.SemaphoreType.DMA
    hbm = pl.BlockSpec(memory_space=pl.ANY)
    fine, e = pl.pallas_call(
        functools.partial(cycle_kernel, nb, ng),
        out_shape=(
            jax.ShapeDtypeStruct((nx, ny, nz), f32),
            jax.ShapeDtypeStruct((cx * cy, cz), f32),
        ),
        in_specs=[hbm] * 3,
        out_specs=(hbm, pl.BlockSpec(memory_space=pltpu.VMEM)),
        scratch_shapes=[
            padded, padded, padded, padded,
            block,
            pltpu.VMEM((nx + 1, ny, nz), f32),
            block, block, block, block, block,
            pltpu.VMEM((4, 2, nx, nz), f32),
            pltpu.VMEM((4, 2, nx, nz), f32),
            pltpu.VMEM((2, nx, nz), f32),
            pltpu.VMEM((2, nx, nz), f32),
            pltpu.VMEM((cx, ny, nz), f32),
            coarse, coarse,
            pltpu.VMEM((ex - 1, ey, cz), f32),
            coarse, coarse, coarse, coarse,
            dma((4,)), dma((4, 4)), dma((4, 4)), dma((2, count)), dma((2, count)),
        ],
        compiler_params=pltpu.CompilerParams(
            collective_id=0, has_side_effects=True, vmem_limit_bytes=40 * 1024 * 1024
        ),
        name="cycle",
    )(right_side, inv_density, pressure)
    return pl.pallas_call(
        expand_kernel,
        grid=(cx,),
        out_shape=jax.ShapeDtypeStruct((nx, ny, nz), f32),
        in_specs=[
            pl.BlockSpec((POOL, ny, nz), lambda g: (g, 0, 0)),
            pl.BlockSpec((cy, cz), lambda g: (g, 0)),
        ],
        out_specs=pl.BlockSpec((POOL, ny, nz), lambda g: (g, 0, 0)),
        name="expand",
    )(fine, e)


def solution(mesh):
    spec = P("box", "group", None)
    return jax.shard_map(
        functools.partial(per_device, mesh.shape["box"], mesh.shape["group"]),
        mesh=mesh,
        in_specs=(spec, spec, spec),
        out_specs=spec,
        check_vma=False,
    )
```

```python
import functools

import jax
import jax.numpy as jnp
from jax import lax
from jax.experimental import pallas as pl
from jax.experimental.pallas import tpu as pltpu
from jax.sharding import PartitionSpec as P

CHEB = 8
POOL = 4
MESH = pl.DeviceIdType.MESH


def chebyshev_factors():
    low, high = 0.05, 2.0
    theta = (high + low) / 2.0
    delta = (high - low) / 2.0
    sigma = theta / delta
    rho = 1.0 / sigma
    steps = []
    for _ in range(CHEB - 1):
        rho_next = 1.0 / (2.0 * sigma - rho)
        steps.append((rho_next * rho, 2.0 * rho_next / delta))
        rho = rho_next
    return 1.0 / theta, steps


def inverse(x):
    r = pl.reciprocal(x, approx=True)
    return r * (2.0 - x * r)


def face(a, b):
    m = a * b
    return (m + m) * inverse(a + b)


def edge_face(a, b):
    m = a * b
    s = a + b
    return jnp.where(m > 0, (m + m) * inverse(s), s)


def split(x):
    hi = x.astype(jnp.bfloat16)
    return hi, (x - hi.astype(jnp.float32)).astype(jnp.bfloat16)


def dot(a, b):
    return jnp.dot(a, b, preferred_element_type=jnp.float32)


def members(rows, cols, long_first):
    r = lax.broadcasted_iota(jnp.int32, (rows, cols), 0)
    c = lax.broadcasted_iota(jnp.int32, (rows, cols), 1)
    same = (r // POOL == c) if long_first else (r == c // POOL)
    return same.astype(jnp.float32).astype(jnp.bfloat16)


def pool(stack):
    g, rows, lanes = stack.shape
    flat = stack.reshape(g * rows, lanes)
    across = members(lanes, lanes // POOL, True)
    hi, lo = split(flat)
    m = dot(hi, across) + dot(lo, across)
    down = members(g * rows // POOL, g * rows, False)
    hi, lo = split(m)
    return (dot(down, hi) + dot(down, lo)) * (1.0 / POOL**3)


def expand(flat, rows):
    lanes = flat.shape[1] * POOL
    across = members(flat.shape[1], lanes, False)
    hi, lo = split(flat)
    wide = dot(hi, across) + dot(lo, across)
    down = members(rows, flat.shape[0], True)
    hi, lo = split(wide)
    return dot(down, hi) + dot(down, lo)


def cycle_kernel(
    nb, ng, f_hbm, b_hbm, p_hbm, fine_hbm, tall_ref,
    V0, B, V1, V2, F, CX, CY, CZ, W, D, T, ysend, yrecv, yface, ygain,
    ACC, GB, GR, KX, KY, KZ, KW, DD,
    lsem, fsend, frecv, csend, crecv,
):
    nx, ny, nz = F.shape
    cx, cy, cz = nx // POOL, ny // POOL, nz // POOL
    hb, hg = (GB.shape[0] // cx - 1) // 2, (GB.shape[1] // cy - 1) // 2
    bx, gx = lax.axis_index("box"), lax.axis_index("group")

    def there(dx, dg):
        ok = (bx + dx >= 0) & (bx + dx < nb)
        return ok & (gx + dg >= 0) & (gx + dg < ng)

    offsets = [
        (dx, dg)
        for dg in range(-hg, hg + 1)
        for dx in range(-hb, hb + 1)
        if (dx, dg) != (0, 0)
    ]
    barrier = pltpu.get_barrier_semaphore()
    for dx, dg in offsets:
        @pl.when(there(dx, dg))
        def _():
            pl.semaphore_signal(
                barrier, inc=1, device_id={"box": bx + dx, "group": gx + dg}, device_id_type=MESH
            )

    inside = pl.ds(1, nx)
    load_b = pltpu.make_async_copy(b_hbm, B.at[inside], lsem.at[0])
    load_p = pltpu.make_async_copy(p_hbm, V0.at[inside], lsem.at[1])
    load_f = pltpu.make_async_copy(f_hbm, F, lsem.at[2])
    load_b.start()
    load_p.start()
    load_f.start()

    fields = [V0, B, V1, V2]
    goes = [(1, 0), (-1, 0), (0, 1), (0, -1)]

    def fine_copy(a, way):
        if way == 0:
            src = (p_hbm, b_hbm)[a].at[nx - 1] if a < 2 else fields[a].at[nx]
            dst = fields[a].at[0]
        elif way == 1:
            src = (p_hbm, b_hbm)[a].at[0] if a < 2 else fields[a].at[1]
            dst = fields[a].at[nx + 1]
        else:
            src, dst = ysend.at[a, 3 - way], yrecv.at[a, way - 2]
        dx, dg = goes[way]
        return pltpu.make_async_remote_copy(
            src_ref=src, dst_ref=dst, send_sem=fsend.at[a, way], recv_sem=frecv.at[a, way],
            device_id={"box": bx + dx, "group": gx + dg}, device_id_type=MESH,
        )

    def send(a, ways):
        for way in ways:
            @pl.when(there(*goes[way]))
            def _():
                fine_copy(a, way).start()

    def receive(a, ways):
        for way in ways:
            @pl.when(there(-goes[way][0], -goes[way][1]))
            def _():
                fine_copy(a, way).wait_recv()

    def coarse_copy(a, o):
        dx, dg = offsets[o]
        G = (GB, GR)[a]
        return pltpu.make_async_remote_copy(
            src_ref=G.at[pl.ds(hb * cx, cx), pl.ds(hg * cy, cy)],
            dst_ref=G.at[pl.ds((hb - dx) * cx, cx), pl.ds((hg - dg) * cy, cy)],
            send_sem=csend.at[a, o], recv_sem=crecv.at[a, o],
            device_id={"box": bx + dx, "group": gx + dg}, device_id_type=MESH,
        )

    def coarse_send(a):
        for o, (dx, dg) in enumerate(offsets):
            @pl.when(there(dx, dg))
            def _():
                coarse_copy(a, o).start()

    def coarse_receive(a):
        for o, (dx, dg) in enumerate(offsets):
            @pl.when(there(-dx, -dg))
            def _():
                coarse_copy(a, o).wait_recv()

    for way in (0, 1):
        @pl.when(jnp.logical_not(there(-goes[way][0], 0)))
        def _():
            for field in fields:
                field[way * (nx + 1)] = jnp.zeros((ny, nz), jnp.float32)
    for way in (2, 3):
        @pl.when(jnp.logical_not(there(0, -goes[way][1])))
        def _():
            for a in range(4):
                yrecv[a, way - 2] = jnp.zeros((nx, nz), jnp.float32)
    for dx, dg in offsets:
        @pl.when(jnp.logical_not(there(dx, dg)))
        def _():
            for G in (GB, GR):
                G[pl.ds((hb + dx) * cx, cx), pl.ds((hg + dg) * cy, cy)] = jnp.zeros(
                    (cx, cy, cz), jnp.float32
                )

    neighbours = 0
    for dx, dg in offsets:
        neighbours = neighbours + there(dx, dg).astype(jnp.int32)
    pl.semaphore_wait(barrier, neighbours)
    send(1, (0, 1))
    send(0, (0, 1))

    def pack(a):
        ysend[a, 0] = fields[a][pl.ds(1, nx), 0, :]
        ysend[a, 1] = fields[a][pl.ds(1, nx), ny - 1, :]

    load_b.wait()
    pack(1)
    send(1, (2, 3))
    load_p.wait()
    pack(0)
    send(0, (2, 3))
    load_f.wait()

    lane = lax.broadcasted_iota(jnp.int32, (ny, nz), 1)
    row = lax.broadcasted_iota(jnp.int32, (ny, nz), 0)
    low_row = lax.broadcasted_iota(jnp.int32, (8, nz), 0) == 0
    high_row = lax.broadcasted_iota(jnp.int32, (8, nz), 0) == 7

    def in_plane(v, ky, kz):
        s = kz * pltpu.roll(v, nz - 1, 1) + pltpu.roll(kz * v, 1, 1)
        return s + (ky * pltpu.roll(v, ny - 1, 0) + pltpu.roll(ky * v, 1, 0))

    def add_rows(t, low, high):
        return jnp.concatenate(
            [
                t[0:8] + jnp.where(low_row, low, 0.0),
                t[8 : ny - 8],
                t[ny - 8 : ny] + jnp.where(high_row, high, 0.0),
            ],
            axis=0,
        )

    def before_halo(i, first=False):
        b, p = B[i + 1], V0[i + 1]
        kz = jnp.where(lane == nz - 1, 0.0, face(b, pltpu.roll(b, nz - 1, 1)))
        ky = jnp.where(row == ny - 1, 0.0, face(b, pltpu.roll(b, ny - 1, 0)))
        CZ[i] = kz
        CY[i] = ky
        if not first:
            CX[i] = face(B[i], b)
        ends = jnp.where((lane == 0) | (lane == nz - 1), b, 0.0)
        D[i] = (kz + pltpu.roll(kz, 1, 1)) + (ky + pltpu.roll(ky, 1, 0)) + ends
        T[i] = F[i] + in_plane(p, ky, kz)

    before_halo(0, True)
    lax.fori_loop(1, nx, lambda i, c: (before_halo(i), c)[1], 0)

    def sum_b(g, c):
        s = B[POOL * g + 1]
        for k in range(1, POOL):
            s = s + B[POOL * g + 1 + k]
        ACC[g] = s
        return c

    lax.fori_loop(0, cx, sum_b, 0)
    center = (pl.ds(hb * cx, cx), pl.ds(hg * cy, cy))
    GB[center] = pool(ACC[...]).reshape(cx, cy, cz)
    coarse_send(0)

    receive(1, (0, 1, 2, 3))
    CX[0] = edge_face(B[0], B[1])
    CX[nx] = edge_face(B[nx], B[nx + 1])
    for side in (0, 1):
        yface[side] = edge_face(ysend[1, side], yrecv[1, side])
    receive(0, (0, 1, 2, 3))

    def gains(a):
        for side in (0, 1):
            ygain[side] = yface[side] * yrecv[a, side]

    gains(0)

    def first_sweep(i):
        at = pl.ds(i, 1)
        k0, k1 = CX[i], CX[i + 1]
        d = add_rows(D[i] + (k0 + k1), yface[0, at, :], yface[1, at, :])
        D[i] = d
        w = (2.0 / 3.0) * inverse(d)
        W[i] = w
        t = T[i] + (k0 * V0[i] + k1 * V0[i + 2])
        t = add_rows(t, ygain[0, at, :], ygain[1, at, :])
        V1[i + 1] = (1.0 / 3.0) * V0[i + 1] + w * t

    def both_ends(step):
        lax.fori_loop(0, 2, lambda j, c: (step(j * (nx - 1)), c)[1], 0)

    def between(step):
        lax.fori_loop(1, nx - 1, lambda i, c: (step(i), c)[1], 0)

    both_ends(first_sweep)
    send(2, (0, 1))
    between(first_sweep)
    pack(2)
    send(2, (2, 3))

    def total(V, i):
        v = V[i + 1]
        x = CX[i] * V[i] + CX[i + 1] * V[i + 2]
        return v, F[i] + x + in_plane(v, CY[i], CZ[i])

    def second_sweep(i):
        v, t = total(V1, i)
        V2[i + 1] = (1.0 / 3.0) * v + W[i] * t

    between(second_sweep)
    receive(2, (0, 1))
    both_ends(second_sweep)
    receive(2, (2, 3))
    gains(2)

    bottom, top = pl.ds(0, 8), pl.ds(ny - 8, 8)

    def second_rows(i, c):
        at = pl.ds(i, 1)
        V2[i + 1, bottom, :] += jnp.where(low_row, W[i, bottom, :] * ygain[0, at, :], 0.0)
        V2[i + 1, top, :] += jnp.where(high_row, W[i, top, :] * ygain[1, at, :], 0.0)
        return c

    lax.fori_loop(0, nx, second_rows, 0)
    send(3, (0, 1))
    pack(3)
    send(3, (2, 3))
    store = pltpu.make_async_copy(V2.at[inside], fine_hbm, lsem.at[3])
    store.start()

    ACC[...] = jnp.zeros_like(ACC)

    def residual(i):
        v, t = total(V2, i)
        ACC[i // POOL] += t - D[i] * v

    between(residual)

    coarse_receive(0)
    gb = GB[...]
    ex, ey, ez = gb.shape
    clane = lax.broadcasted_iota(jnp.int32, gb.shape, 2)
    kx = edge_face(gb[:-1], gb[1:])
    ky = edge_face(gb, pltpu.roll(gb, ey - 1, 1))
    kz = jnp.where(clane == ez - 1, 0.0, edge_face(gb, pltpu.roll(gb, ez - 1, 2)))
    KX[...] = kx
    KY[...] = ky
    KZ[...] = kz
    ends = jnp.where((clane == 0) | (clane == ez - 1), gb, 0.0)
    d = (kz + pltpu.roll(kz, 1, 2)) + (ky + pltpu.roll(ky, 1, 1)) + ends
    d = d[1:-1] + (kx[:-1] + kx[1:])
    KW[pl.ds(1, ex - 2)] = jnp.where(gb[1:-1] > 0, inverse(d), 0.0)

    receive(3, (0, 1))
    both_ends(residual)
    receive(3, (2, 3))
    gains(3)

    def residual_rows(i, c):
        at, g = pl.ds(i, 1), i // POOL
        ACC[g, bottom, :] += jnp.where(low_row, ygain[0, at, :], 0.0)
        ACC[g, top, :] += jnp.where(high_row, ygain[1, at, :], 0.0)
        return c

    lax.fori_loop(0, nx, residual_rows, 0)
    GR[center] = pool(ACC[...]).reshape(cx, cy, cz)
    coarse_send(1)
    coarse_receive(1)

    start, steps = chebyshev_factors()
    lo, hi = 1, ex - 1
    q = GR[pl.ds(lo, hi - lo)] * KW[pl.ds(lo, hi - lo)] * 16.0
    d = q * start
    DD[pl.ds(lo, hi - lo)] = d
    e = DD[center]
    for decay, gain in steps:
        lo, hi = lo + 1, hi - 1
        span = pl.ds(lo, hi - lo)
        v = DD[span]
        ky, kz = KY[span], KZ[span]
        s = KX[pl.ds(lo - 1, hi - lo)] * DD[pl.ds(lo - 1, hi - lo)]
        s = s + KX[span] * DD[pl.ds(lo + 1, hi - lo)]
        s = s + (ky * pltpu.roll(v, ey - 1, 1) + pltpu.roll(ky * v, 1, 1))
        s = s + (kz * pltpu.roll(v, ez - 1, 2) + pltpu.roll(kz * v, 1, 2))
        q = q[1:-1] - v + KW[span] * s
        DD[span] = decay * v + gain * q
        e = e + DD[center]
    tall_ref[...] = expand(e.reshape(cx * cy, cz), cx * ny).reshape(cx, 1, ny, nz)

    for a in range(4):
        for way in range(4):
            @pl.when(there(*goes[way]))
            def _():
                fine_copy(a, way).wait_send()
    for a in range(2):
        for o, (dx, dg) in enumerate(offsets):
            @pl.when(there(dx, dg))
            def _():
                coarse_copy(a, o).wait_send()
    store.wait()


def per_device(nb, ng, right_side, inv_density, pressure):
    nx, ny, nz = right_side.shape
    cx, cy, cz = nx // POOL, ny // POOL, nz // POOL
    hb, hg = -(-CHEB // cx), -(-CHEB // cy)
    ex, ey = (2 * hb + 1) * cx, (2 * hg + 1) * cy
    count = (2 * hb + 1) * (2 * hg + 1) - 1
    f32 = jnp.float32
    block = pltpu.VMEM((nx, ny, nz), f32)
    padded = pltpu.VMEM((nx + 2, ny, nz), f32)
    coarse = pltpu.VMEM((ex, ey, cz), f32)
    dma = pltpu.SemaphoreType.DMA
    hbm = pl.BlockSpec(memory_space=pltpu.HBM)
    fine, tall = pl.pallas_call(
        functools.partial(cycle_kernel, nb, ng),
        out_shape=(
            jax.ShapeDtypeStruct((nx, ny, nz), f32),
            jax.ShapeDtypeStruct((cx, 1, ny, nz), f32),
        ),
        in_specs=[hbm] * 3,
        out_specs=(pl.BlockSpec(memory_space=pl.ANY), pl.BlockSpec(memory_space=pltpu.VMEM)),
        scratch_shapes=[
            padded, padded, padded, padded,
            block,
            pltpu.VMEM((nx + 1, ny, nz), f32),
            block, block, block, block, block,
            pltpu.VMEM((4, 2, nx, nz), f32),
            pltpu.VMEM((4, 2, nx, nz), f32),
            pltpu.VMEM((2, nx, nz), f32),
            pltpu.VMEM((2, nx, nz), f32),
            pltpu.VMEM((cx, ny, nz), f32),
            coarse, coarse,
            pltpu.VMEM((ex - 1, ey, cz), f32),
            coarse, coarse, coarse, coarse,
            dma((4,)), dma((4, 4)), dma((4, 4)), dma((2, count)), dma((2, count)),
        ],
        compiler_params=pltpu.CompilerParams(
            collective_id=0, has_side_effects=True, vmem_limit_bytes=63 * 1024 * 1024
        ),
        name="cycle",
    )(right_side, inv_density, pressure)
    return (fine.reshape(cx, POOL, ny, nz) + tall).reshape(nx, ny, nz)


def solution(mesh):
    spec = P("box", "group", None)
    return jax.shard_map(
        functools.partial(per_device, mesh.shape["box"], mesh.shape["group"]),
        mesh=mesh,
        in_specs=(spec, spec, spec),
        out_specs=spec,
        check_vma=False,
    )
```

```python
import functools

import jax
import jax.numpy as jnp
from jax import lax
from jax.experimental import pallas as pl
from jax.experimental.pallas import tpu as pltpu
from jax.sharding import PartitionSpec as P

CHEB = 8
POOL = 4
MESH = pl.DeviceIdType.MESH


def chebyshev_factors():
    low, high = 0.05, 2.0
    theta = (high + low) / 2.0
    delta = (high - low) / 2.0
    sigma = theta / delta
    rho = 1.0 / sigma
    steps = []
    for _ in range(CHEB - 1):
        rho_next = 1.0 / (2.0 * sigma - rho)
        steps.append((rho_next * rho, 2.0 * rho_next / delta))
        rho = rho_next
    return 1.0 / theta, steps


def inverse(x):
    r = pl.reciprocal(x, approx=True)
    return r * (2.0 - x * r)


def face(a, b):
    m = a * b
    return (m + m) * inverse(a + b)


def edge_face(a, b):
    m = a * b
    s = a + b
    return jnp.where(m > 0, (m + m) * inverse(s), s)


def split(x):
    hi = x.astype(jnp.bfloat16)
    return hi, (x - hi.astype(jnp.float32)).astype(jnp.bfloat16)


def dot(a, b):
    return jnp.dot(a, b, preferred_element_type=jnp.float32)


def members(rows, cols, long_first):
    r = lax.broadcasted_iota(jnp.int32, (rows, cols), 0)
    c = lax.broadcasted_iota(jnp.int32, (rows, cols), 1)
    same = (r // POOL == c) if long_first else (r == c // POOL)
    return same.astype(jnp.float32).astype(jnp.bfloat16)


def pool(stack):
    g, rows, lanes = stack.shape
    flat = stack.reshape(g * rows, lanes)
    across = members(lanes, lanes // POOL, True)
    hi, lo = split(flat)
    m = dot(hi, across) + dot(lo, across)
    down = members(g * rows // POOL, g * rows, False)
    hi, lo = split(m)
    return (dot(down, hi) + dot(down, lo)) * (1.0 / POOL**3)


def expand(flat, rows):
    lanes = flat.shape[1] * POOL
    across = members(flat.shape[1], lanes, False)
    hi, lo = split(flat)
    wide = dot(hi, across) + dot(lo, across)
    down = members(rows, flat.shape[0], True)
    hi, lo = split(wide)
    return dot(down, hi) + dot(down, lo)


def cycle_kernel(
    nb, ng, f_hbm, b_hbm, p_hbm, out_hbm,
    V0, B, V1, V2, F, CX, CY, CZ, W, D, T, ysend, yrecv, yface, ygain,
    ACC, GB, GR, KX, KY, KZ, KW, DD,
    lsem, fsend, frecv, csend, crecv,
):
    nx, ny, nz = F.shape
    cx, cy, cz = nx // POOL, ny // POOL, nz // POOL
    hb, hg = (GB.shape[0] // cx - 1) // 2, (GB.shape[1] // cy - 1) // 2
    bx, gx = lax.axis_index("box"), lax.axis_index("group")

    def there(dx, dg):
        ok = (bx + dx >= 0) & (bx + dx < nb)
        return ok & (gx + dg >= 0) & (gx + dg < ng)

    offsets = [
        (dx, dg)
        for dg in range(-hg, hg + 1)
        for dx in range(-hb, hb + 1)
        if (dx, dg) != (0, 0)
    ]
    barrier = pltpu.get_barrier_semaphore()
    for dx, dg in offsets:
        @pl.when(there(dx, dg))
        def _():
            pl.semaphore_signal(
                barrier, inc=1, device_id={"box": bx + dx, "group": gx + dg}, device_id_type=MESH
            )

    inside = pl.ds(1, nx)
    load_b = pltpu.make_async_copy(b_hbm, B.at[inside], lsem.at[0])
    load_p = pltpu.make_async_copy(p_hbm, V0.at[inside], lsem.at[1])
    load_f = pltpu.make_async_copy(f_hbm, F, lsem.at[2])
    load_b.start()
    load_p.start()
    load_f.start()

    fields = [V0, B, V1, V2]
    goes = [(1, 0), (-1, 0), (0, 1), (0, -1)]

    def fine_copy(a, way):
        if way == 0:
            src = (p_hbm, b_hbm)[a].at[nx - 1] if a < 2 else fields[a].at[nx]
            dst = fields[a].at[0]
        elif way == 1:
            src = (p_hbm, b_hbm)[a].at[0] if a < 2 else fields[a].at[1]
            dst = fields[a].at[nx + 1]
        else:
            src, dst = ysend.at[a, 3 - way], yrecv.at[a, way - 2]
        dx, dg = goes[way]
        return pltpu.make_async_remote_copy(
            src_ref=src, dst_ref=dst, send_sem=fsend.at[a, way], recv_sem=frecv.at[a, way],
            device_id={"box": bx + dx, "group": gx + dg}, device_id_type=MESH,
        )

    def send(a, ways):
        for way in ways:
            @pl.when(there(*goes[way]))
            def _():
                fine_copy(a, way).start()

    def receive(a, ways):
        for way in ways:
            @pl.when(there(-goes[way][0], -goes[way][1]))
            def _():
                fine_copy(a, way).wait_recv()

    def needed(a, dx, dg):
        reach = (CHEB, CHEB - 1)[a]
        if dg:
            reach = reach - (abs(dg) - 1) * cy - 1
        return min(cx, reach - (abs(dx) - 1) * cx) if dx else cx

    def coarse_copy(a, o):
        dx, dg = offsets[o]
        G = (GB, GR)[a]
        n = needed(a, dx, dg)
        skip = cx - n if dx > 0 else 0
        return pltpu.make_async_remote_copy(
            src_ref=G.at[pl.ds(hb * cx + skip, n), pl.ds(hg * cy, cy)],
            dst_ref=G.at[pl.ds((hb - dx) * cx + skip, n), pl.ds((hg - dg) * cy, cy)],
            send_sem=csend.at[a, o], recv_sem=crecv.at[a, o],
            device_id={"box": bx + dx, "group": gx + dg}, device_id_type=MESH,
        )

    def coarse_send(a):
        for o, (dx, dg) in enumerate(offsets):
            @pl.when(there(dx, dg))
            def _():
                coarse_copy(a, o).start()

    def coarse_receive(a):
        for o, (dx, dg) in enumerate(offsets):
            @pl.when(there(-dx, -dg))
            def _():
                coarse_copy(a, o).wait_recv()

    for way in (0, 1):
        @pl.when(jnp.logical_not(there(-goes[way][0], 0)))
        def _():
            for field in fields:
                field[way * (nx + 1)] = jnp.zeros((ny, nz), jnp.float32)
    for way in (2, 3):
        @pl.when(jnp.logical_not(there(0, -goes[way][1])))
        def _():
            for a in range(4):
                yrecv[a, way - 2] = jnp.zeros((nx, nz), jnp.float32)
    for dx, dg in offsets:
        @pl.when(jnp.logical_not(there(dx, dg)))
        def _():
            for G in (GB, GR):
                G[pl.ds((hb + dx) * cx, cx), pl.ds((hg + dg) * cy, cy)] = jnp.zeros(
                    (cx, cy, cz), jnp.float32
                )

    for a, G in enumerate((GB, GR)):
        for dx, dg in offsets:
            rest = cx - needed(a, dx, dg)
            if rest:
                G[
                    pl.ds((hb + dx) * cx + (cx - rest if dx > 0 else 0), rest),
                    pl.ds((hg + dg) * cy, cy),
                ] = jnp.zeros((rest, cy, cz), jnp.float32)

    neighbours = 0
    for dx, dg in offsets:
        neighbours = neighbours + there(dx, dg).astype(jnp.int32)
    pl.semaphore_wait(barrier, neighbours)
    send(1, (0, 1))
    send(0, (0, 1))

    def pack(a):
        ysend[a, 0] = fields[a][pl.ds(1, nx), 0, :]
        ysend[a, 1] = fields[a][pl.ds(1, nx), ny - 1, :]

    load_b.wait()
    pack(1)
    send(1, (2, 3))
    load_p.wait()
    pack(0)
    send(0, (2, 3))
    load_f.wait()

    lane = lax.broadcasted_iota(jnp.int32, (ny, nz), 1)
    row = lax.broadcasted_iota(jnp.int32, (ny, nz), 0)
    low_row = lax.broadcasted_iota(jnp.int32, (8, nz), 0) == 0
    high_row = lax.broadcasted_iota(jnp.int32, (8, nz), 0) == 7

    def in_plane(v, ky, kz):
        s = kz * pltpu.roll(v, nz - 1, 1) + pltpu.roll(kz * v, 1, 1)
        return s + (ky * pltpu.roll(v, ny - 1, 0) + pltpu.roll(ky * v, 1, 0))

    def add_rows(t, low, high):
        return jnp.concatenate(
            [
                t[0:8] + jnp.where(low_row, low, 0.0),
                t[8 : ny - 8],
                t[ny - 8 : ny] + jnp.where(high_row, high, 0.0),
            ],
            axis=0,
        )

    def before_halo(i, first=False):
        b, p = B[i + 1], V0[i + 1]
        kz = jnp.where(lane == nz - 1, 0.0, face(b, pltpu.roll(b, nz - 1, 1)))
        ky = jnp.where(row == ny - 1, 0.0, face(b, pltpu.roll(b, ny - 1, 0)))
        CZ[i] = kz
        CY[i] = ky
        if not first:
            CX[i] = face(B[i], b)
        ends = jnp.where((lane == 0) | (lane == nz - 1), b, 0.0)
        D[i] = (kz + pltpu.roll(kz, 1, 1)) + (ky + pltpu.roll(ky, 1, 0)) + ends
        T[i] = F[i] + in_plane(p, ky, kz)

    before_halo(0, True)
    lax.fori_loop(1, nx, lambda i, c: (before_halo(i), c)[1], 0)

    def sum_b(g, c):
        s = B[POOL * g + 1]
        for k in range(1, POOL):
            s = s + B[POOL * g + 1 + k]
        ACC[g] = s
        return c

    lax.fori_loop(0, cx, sum_b, 0)
    center = (pl.ds(hb * cx, cx), pl.ds(hg * cy, cy))
    GB[center] = pool(ACC[...]).reshape(cx, cy, cz)
    coarse_send(0)

    def inner_sweep(i):
        k0, k1 = CX[i], CX[i + 1]
        d = D[i] + (k0 + k1)
        D[i] = d
        w = (2.0 / 3.0) * inverse(d)
        W[i] = w
        t = T[i] + (k0 * V0[i] + k1 * V0[i + 2])
        T[i] = t
        V1[i + 1] = (1.0 / 3.0) * V0[i + 1] + w * t

    def both_ends(step):
        lax.fori_loop(0, 2, lambda j, c: (step(j * (nx - 1)), c)[1], 0)

    def between(step):
        lax.fori_loop(1, nx - 1, lambda i, c: (step(i), c)[1], 0)

    bottom, top = pl.ds(0, 8), pl.ds(ny - 8, 8)
    between(inner_sweep)

    receive(1, (0, 1, 2, 3))
    CX[0] = edge_face(B[0], B[1])
    CX[nx] = edge_face(B[nx], B[nx + 1])
    for side in (0, 1):
        yface[side] = edge_face(ysend[1, side], yrecv[1, side])
    receive(0, (0, 1, 2, 3))

    def gains(a):
        for side in (0, 1):
            ygain[side] = yface[side] * yrecv[a, side]

    gains(0)

    def first_sweep(i):
        at = pl.ds(i, 1)
        k0, k1 = CX[i], CX[i + 1]
        d = add_rows(D[i] + (k0 + k1), yface[0, at, :], yface[1, at, :])
        D[i] = d
        w = (2.0 / 3.0) * inverse(d)
        W[i] = w
        t = T[i] + (k0 * V0[i] + k1 * V0[i + 2])
        t = add_rows(t, ygain[0, at, :], ygain[1, at, :])
        V1[i + 1] = (1.0 / 3.0) * V0[i + 1] + w * t

    def edge_sweep(i):
        at = pl.ds(i, 1)
        for side, rows, mask in ((0, bottom, low_row), (1, top, high_row)):
            d = D[i, rows, :] + jnp.where(mask, yface[side, at, :], 0.0)
            D[i, rows, :] = d
            w = (2.0 / 3.0) * inverse(d)
            W[i, rows, :] = w
            t = T[i, rows, :] + jnp.where(mask, ygain[side, at, :], 0.0)
            V1[i + 1, rows, :] = (1.0 / 3.0) * V0[i + 1, rows, :] + w * t

    both_ends(first_sweep)
    send(2, (0, 1))
    between(edge_sweep)
    pack(2)
    send(2, (2, 3))

    def total(V, i):
        v = V[i + 1]
        x = CX[i] * V[i] + CX[i + 1] * V[i + 2]
        return v, F[i] + x + in_plane(v, CY[i], CZ[i])

    def second_sweep(i):
        v, t = total(V1, i)
        V2[i + 1] = (1.0 / 3.0) * v + W[i] * t

    between(second_sweep)
    receive(2, (0, 1))
    both_ends(second_sweep)
    receive(2, (2, 3))
    gains(2)

    def second_rows(i, c):
        at = pl.ds(i, 1)
        V2[i + 1, bottom, :] += jnp.where(low_row, W[i, bottom, :] * ygain[0, at, :], 0.0)
        V2[i + 1, top, :] += jnp.where(high_row, W[i, top, :] * ygain[1, at, :], 0.0)
        return c

    lax.fori_loop(0, nx, second_rows, 0)
    send(3, (0, 1))
    pack(3)
    send(3, (2, 3))

    ACC[...] = jnp.zeros_like(ACC)

    def residual(i):
        v, t = total(V2, i)
        ACC[i // POOL] += t - D[i] * v

    between(residual)

    coarse_receive(0)
    gb = GB[...]
    ex, ey, ez = gb.shape
    clane = lax.broadcasted_iota(jnp.int32, gb.shape, 2)
    kx = edge_face(gb[:-1], gb[1:])
    ky = edge_face(gb, pltpu.roll(gb, ey - 1, 1))
    kz = jnp.where(clane == ez - 1, 0.0, edge_face(gb, pltpu.roll(gb, ez - 1, 2)))
    KX[...] = kx
    KY[...] = ky
    KZ[...] = kz
    ends = jnp.where((clane == 0) | (clane == ez - 1), gb, 0.0)
    d = (kz + pltpu.roll(kz, 1, 2)) + (ky + pltpu.roll(ky, 1, 1)) + ends
    d = d[1:-1] + (kx[:-1] + kx[1:])
    KW[pl.ds(1, ex - 2)] = jnp.where(gb[1:-1] > 0, inverse(d), 0.0)

    receive(3, (0, 1))
    both_ends(residual)
    receive(3, (2, 3))
    gains(3)

    def residual_rows(i, c):
        at, g = pl.ds(i, 1), i // POOL
        ACC[g, bottom, :] += jnp.where(low_row, ygain[0, at, :], 0.0)
        ACC[g, top, :] += jnp.where(high_row, ygain[1, at, :], 0.0)
        return c

    lax.fori_loop(0, nx, residual_rows, 0)
    GR[center] = pool(ACC[...]).reshape(cx, cy, cz)
    coarse_send(1)
    coarse_receive(1)

    start, steps = chebyshev_factors()
    lo, hi = 1, ex - 1
    q = GR[pl.ds(lo, hi - lo)] * KW[pl.ds(lo, hi - lo)] * 16.0
    d = q * start
    DD[pl.ds(lo, hi - lo)] = d
    e = DD[center]
    for decay, gain in steps:
        lo, hi = lo + 1, hi - 1
        span = pl.ds(lo, hi - lo)
        v = DD[span]
        ky, kz = KY[span], KZ[span]
        s = KX[pl.ds(lo - 1, hi - lo)] * DD[pl.ds(lo - 1, hi - lo)]
        s = s + KX[span] * DD[pl.ds(lo + 1, hi - lo)]
        s = s + (ky * pltpu.roll(v, ey - 1, 1) + pltpu.roll(ky * v, 1, 1))
        s = s + (kz * pltpu.roll(v, ez - 1, 2) + pltpu.roll(kz * v, 1, 2))
        q = q[1:-1] - v + KW[span] * s
        DD[span] = decay * v + gain * q
        e = e + DD[center]
    ACC[...] = expand(e.reshape(cx * cy, cz), cx * ny).reshape(cx, ny, nz)
    stores = []
    for g in range(cx):
        tall = ACC[g]
        for k in range(POOL * g, POOL * (g + 1)):
            T[k] = V2[k + 1] + tall
        planes = pl.ds(POOL * g, POOL)
        stores.append(pltpu.make_async_copy(T.at[planes], out_hbm.at[planes], lsem.at[3 + g]))
        stores[-1].start()

    for a in range(4):
        for way in range(4):
            @pl.when(there(*goes[way]))
            def _():
                fine_copy(a, way).wait_send()
    for a in range(2):
        for o, (dx, dg) in enumerate(offsets):
            @pl.when(there(dx, dg))
            def _():
                coarse_copy(a, o).wait_send()
    for store in stores:
        store.wait()


def per_device(nb, ng, right_side, inv_density, pressure):
    nx, ny, nz = right_side.shape
    cx, cy, cz = nx // POOL, ny // POOL, nz // POOL
    hb, hg = -(-CHEB // cx), -(-CHEB // cy)
    ex, ey = (2 * hb + 1) * cx, (2 * hg + 1) * cy
    count = (2 * hb + 1) * (2 * hg + 1) - 1
    f32 = jnp.float32
    block = pltpu.VMEM((nx, ny, nz), f32)
    padded = pltpu.VMEM((nx + 2, ny, nz), f32)
    coarse = pltpu.VMEM((ex, ey, cz), f32)
    dma = pltpu.SemaphoreType.DMA
    hbm = pl.BlockSpec(memory_space=pltpu.HBM)
    return pl.pallas_call(
        functools.partial(cycle_kernel, nb, ng),
        out_shape=jax.ShapeDtypeStruct((nx, ny, nz), f32),
        in_specs=[hbm] * 3,
        out_specs=pl.BlockSpec(memory_space=pl.ANY),
        scratch_shapes=[
            padded, padded, padded, padded,
            block,
            pltpu.VMEM((nx + 1, ny, nz), f32),
            block, block, block, block, block,
            pltpu.VMEM((4, 2, nx, nz), f32),
            pltpu.VMEM((4, 2, nx, nz), f32),
            pltpu.VMEM((2, nx, nz), f32),
            pltpu.VMEM((2, nx, nz), f32),
            pltpu.VMEM((cx, ny, nz), f32),
            coarse, coarse,
            pltpu.VMEM((ex - 1, ey, cz), f32),
            coarse, coarse, coarse, coarse,
            dma((3 + cx,)), dma((4, 4)), dma((4, 4)), dma((2, count)), dma((2, count)),
        ],
        compiler_params=pltpu.CompilerParams(
            collective_id=0, has_side_effects=True, vmem_limit_bytes=63 * 1024 * 1024
        ),
        name="cycle",
    )(right_side, inv_density, pressure)


def solution(mesh):
    spec = P("box", "group", None)
    return jax.shard_map(
        functools.partial(per_device, mesh.shape["box"], mesh.shape["group"]),
        mesh=mesh,
        in_specs=(spec, spec, spec),
        out_specs=spec,
        check_vma=False,
    )
```

```python
import functools

import jax
import jax.numpy as jnp
from jax import lax
from jax.experimental import pallas as pl
from jax.experimental.pallas import tpu as pltpu
from jax.sharding import PartitionSpec as P

CHEB = 8
POOL = 4
MESH = pl.DeviceIdType.MESH


def chebyshev_factors():
    low, high = 0.05, 2.0
    theta = (high + low) / 2.0
    delta = (high - low) / 2.0
    sigma = theta / delta
    rho = 1.0 / sigma
    steps = []
    for _ in range(CHEB - 1):
        rho_next = 1.0 / (2.0 * sigma - rho)
        steps.append((rho_next * rho, 2.0 * rho_next / delta))
        rho = rho_next
    return 1.0 / theta, steps


def inverse(x):
    r = pl.reciprocal(x, approx=True)
    return r * (2.0 - x * r)


def face(a, b):
    m = a * b
    return (m + m) * inverse(a + b)


def edge_face(a, b):
    m = a * b
    s = a + b
    return jnp.where(m > 0, (m + m) * inverse(s), s)


def split(x):
    hi = x.astype(jnp.bfloat16)
    return hi, (x - hi.astype(jnp.float32)).astype(jnp.bfloat16)


def dot(a, b):
    return jnp.dot(a, b, preferred_element_type=jnp.float32)


def members(rows, cols, long_first):
    r = lax.broadcasted_iota(jnp.int32, (rows, cols), 0)
    c = lax.broadcasted_iota(jnp.int32, (rows, cols), 1)
    same = (r // POOL == c) if long_first else (r == c // POOL)
    return same.astype(jnp.float32).astype(jnp.bfloat16)


def pool(stack):
    g, rows, lanes = stack.shape
    flat = stack.reshape(g * rows, lanes)
    across = members(lanes, lanes // POOL, True)
    hi, lo = split(flat)
    m = dot(hi, across) + dot(lo, across)
    down = members(g * rows // POOL, g * rows, False)
    hi, lo = split(m)
    return (dot(down, hi) + dot(down, lo)) * (1.0 / POOL**3)


def expand(flat, rows):
    lanes = flat.shape[1] * POOL
    across = members(flat.shape[1], lanes, False)
    hi, lo = split(flat)
    wide = dot(hi, across) + dot(lo, across)
    down = members(rows, flat.shape[0], True)
    hi, lo = split(wide)
    return dot(down, hi) + dot(down, lo)


def cycle_kernel(
    nb, ng, f_hbm, b_hbm, p_hbm, out_hbm,
    V0, B, V1, V2, F, CX, CY, CZ, W, D, T, ysend, yrecv, yface, ygain,
    ACC, GB, GR, KX, KY, KZ, KW, DD,
    lsem, fsend, frecv, csend, crecv,
):
    nx, ny, nz = F.shape
    cx, cy, cz = nx // POOL, ny // POOL, nz // POOL
    hb, hg = (GB.shape[0] // cx - 1) // 2, (GB.shape[1] // cy - 1) // 2
    bx, gx = lax.axis_index("box"), lax.axis_index("group")

    def there(dx, dg):
        ok = (bx + dx >= 0) & (bx + dx < nb)
        return ok & (gx + dg >= 0) & (gx + dg < ng)

    offsets = [
        (dx, dg)
        for dg in range(-hg, hg + 1)
        for dx in range(-hb, hb + 1)
        if (dx, dg) != (0, 0)
    ]
    barrier = pltpu.get_barrier_semaphore()
    for dx, dg in offsets:
        @pl.when(there(dx, dg))
        def _():
            pl.semaphore_signal(
                barrier, inc=1, device_id={"box": bx + dx, "group": gx + dg}, device_id_type=MESH
            )

    inside = pl.ds(1, nx)
    load_b = pltpu.make_async_copy(b_hbm, B.at[inside], lsem.at[0])
    load_p = pltpu.make_async_copy(p_hbm, V0.at[inside], lsem.at[1])
    load_f = pltpu.make_async_copy(f_hbm, F, lsem.at[2])
    load_b.start()
    load_p.start()
    load_f.start()

    fields = [V0, B, V1, V2]
    goes = [(1, 0), (-1, 0), (0, 1), (0, -1)]

    def fine_copy(a, way):
        if way == 0:
            src = (p_hbm, b_hbm)[a].at[nx - 1] if a < 2 else fields[a].at[nx]
            dst = fields[a].at[0]
        elif way == 1:
            src = (p_hbm, b_hbm)[a].at[0] if a < 2 else fields[a].at[1]
            dst = fields[a].at[nx + 1]
        else:
            src, dst = ysend.at[a, 3 - way], yrecv.at[a, way - 2]
        dx, dg = goes[way]
        return pltpu.make_async_remote_copy(
            src_ref=src, dst_ref=dst, send_sem=fsend.at[a, way], recv_sem=frecv.at[a, way],
            device_id={"box": bx + dx, "group": gx + dg}, device_id_type=MESH,
        )

    def send(a, ways):
        for way in ways:
            @pl.when(there(*goes[way]))
            def _():
                fine_copy(a, way).start()

    def receive(a, ways):
        for way in ways:
            @pl.when(there(-goes[way][0], -goes[way][1]))
            def _():
                fine_copy(a, way).wait_recv()

    def needed(a, dx, dg):
        reach = (CHEB, CHEB - 1)[a]
        if dg:
            reach = reach - (abs(dg) - 1) * cy - 1
        return min(cx, reach - (abs(dx) - 1) * cx) if dx else cx

    def coarse_copy(a, o):
        dx, dg = offsets[o]
        G = (GB, GR)[a]
        n = needed(a, dx, dg)
        skip = cx - n if dx > 0 else 0
        return pltpu.make_async_remote_copy(
            src_ref=G.at[pl.ds(hb * cx + skip, n), pl.ds(hg * cy, cy)],
            dst_ref=G.at[pl.ds((hb - dx) * cx + skip, n), pl.ds((hg - dg) * cy, cy)],
            send_sem=csend.at[a, o], recv_sem=crecv.at[a, o],
            device_id={"box": bx + dx, "group": gx + dg}, device_id_type=MESH,
        )

    def coarse_send(a):
        for o, (dx, dg) in enumerate(offsets):
            @pl.when(there(dx, dg))
            def _():
                coarse_copy(a, o).start()

    def coarse_receive(a):
        for o, (dx, dg) in enumerate(offsets):
            @pl.when(there(-dx, -dg))
            def _():
                coarse_copy(a, o).wait_recv()

    for way in (0, 1):
        @pl.when(jnp.logical_not(there(-goes[way][0], 0)))
        def _():
            for field in fields:
                field[way * (nx + 1)] = jnp.zeros((ny, nz), jnp.float32)
    for way in (2, 3):
        @pl.when(jnp.logical_not(there(0, -goes[way][1])))
        def _():
            for a in range(4):
                yrecv[a, way - 2] = jnp.zeros((nx, nz), jnp.float32)
    for dx, dg in offsets:
        @pl.when(jnp.logical_not(there(dx, dg)))
        def _():
            for G in (GB, GR):
                G[pl.ds((hb + dx) * cx, cx), pl.ds((hg + dg) * cy, cy)] = jnp.zeros(
                    (cx, cy, cz), jnp.float32
                )

    for a, G in enumerate((GB, GR)):
        for dx, dg in offsets:
            rest = cx - needed(a, dx, dg)
            if rest:
                G[
                    pl.ds((hb + dx) * cx + (cx - rest if dx > 0 else 0), rest),
                    pl.ds((hg + dg) * cy, cy),
                ] = jnp.zeros((rest, cy, cz), jnp.float32)

    neighbours = 0
    for dx, dg in offsets:
        neighbours = neighbours + there(dx, dg).astype(jnp.int32)
    pl.semaphore_wait(barrier, neighbours)
    send(1, (0, 1))
    send(0, (0, 1))

    def pack(a):
        ysend[a, 0] = fields[a][pl.ds(1, nx), 0, :]
        ysend[a, 1] = fields[a][pl.ds(1, nx), ny - 1, :]

    load_b.wait()
    pack(1)
    send(1, (2, 3))
    load_p.wait()
    pack(0)
    send(0, (2, 3))
    load_f.wait()

    lane = lax.broadcasted_iota(jnp.int32, (ny, nz), 1)
    row = lax.broadcasted_iota(jnp.int32, (ny, nz), 0)
    low_row = lax.broadcasted_iota(jnp.int32, (8, nz), 0) == 0
    high_row = lax.broadcasted_iota(jnp.int32, (8, nz), 0) == 7

    def in_plane(v, ky, kz):
        s = kz * pltpu.roll(v, nz - 1, 1) + pltpu.roll(kz * v, 1, 1)
        return s + (ky * pltpu.roll(v, ny - 1, 0) + pltpu.roll(ky * v, 1, 0))

    def add_rows(t, low, high):
        return jnp.concatenate(
            [
                t[0:8] + jnp.where(low_row, low, 0.0),
                t[8 : ny - 8],
                t[ny - 8 : ny] + jnp.where(high_row, high, 0.0),
            ],
            axis=0,
        )

    def before_halo(i, first=False):
        b, p = B[i + 1], V0[i + 1]
        kz = jnp.where(lane == nz - 1, 0.0, face(b, pltpu.roll(b, nz - 1, 1)))
        ky = jnp.where(row == ny - 1, 0.0, face(b, pltpu.roll(b, ny - 1, 0)))
        CZ[i] = kz
        CY[i] = ky
        if not first:
            CX[i] = face(B[i], b)
        ends = jnp.where((lane == 0) | (lane == nz - 1), b, 0.0)
        D[i] = (kz + pltpu.roll(kz, 1, 1)) + (ky + pltpu.roll(ky, 1, 0)) + ends
        T[i] = F[i] + in_plane(p, ky, kz)

    before_halo(0, True)
    lax.fori_loop(1, nx, lambda i, c: (before_halo(i), c)[1], 0)

    def sum_b(g, c):
        s = B[POOL * g + 1]
        for k in range(1, POOL):
            s = s + B[POOL * g + 1 + k]
        ACC[g] = s
        return c

    lax.fori_loop(0, cx, sum_b, 0)
    center = (pl.ds(hb * cx, cx), pl.ds(hg * cy, cy))
    GB[center] = pool(ACC[...]).reshape(cx, cy, cz)
    coarse_send(0)

    def inner_sweep(i):
        k0, k1 = CX[i], CX[i + 1]
        d = D[i] + (k0 + k1)
        D[i] = d
        w = (2.0 / 3.0) * inverse(d)
        W[i] = w
        t = T[i] + (k0 * V0[i] + k1 * V0[i + 2])
        T[i] = t
        V1[i + 1] = (1.0 / 3.0) * V0[i + 1] + w * t

    def both_ends(step):
        lax.fori_loop(0, 2, lambda j, c: (step(j * (nx - 1)), c)[1], 0)

    def between(step):
        lax.fori_loop(1, nx - 1, lambda i, c: (step(i), c)[1], 0)

    bottom, top = pl.ds(0, 8), pl.ds(ny - 8, 8)
    between(inner_sweep)

    receive(1, (0, 1, 2, 3))
    CX[0] = edge_face(B[0], B[1])
    CX[nx] = edge_face(B[nx], B[nx + 1])
    for side in (0, 1):
        yface[side] = edge_face(ysend[1, side], yrecv[1, side])
    receive(0, (0, 1, 2, 3))

    def gains(a):
        for side in (0, 1):
            ygain[side] = yface[side] * yrecv[a, side]

    gains(0)

    def first_sweep(i):
        at = pl.ds(i, 1)
        k0, k1 = CX[i], CX[i + 1]
        d = add_rows(D[i] + (k0 + k1), yface[0, at, :], yface[1, at, :])
        D[i] = d
        w = (2.0 / 3.0) * inverse(d)
        W[i] = w
        t = T[i] + (k0 * V0[i] + k1 * V0[i + 2])
        t = add_rows(t, ygain[0, at, :], ygain[1, at, :])
        V1[i + 1] = (1.0 / 3.0) * V0[i + 1] + w * t

    def edge_sweep(i):
        at = pl.ds(i, 1)
        for side, rows, mask in ((0, bottom, low_row), (1, top, high_row)):
            d = D[i, rows, :] + jnp.where(mask, yface[side, at, :], 0.0)
            D[i, rows, :] = d
            w = (2.0 / 3.0) * inverse(d)
            W[i, rows, :] = w
            t = T[i, rows, :] + jnp.where(mask, ygain[side, at, :], 0.0)
            V1[i + 1, rows, :] = (1.0 / 3.0) * V0[i + 1, rows, :] + w * t

    both_ends(first_sweep)
    send(2, (0, 1))
    between(edge_sweep)
    pack(2)
    send(2, (2, 3))

    def total(V, i):
        v = V[i + 1]
        x = CX[i] * V[i] + CX[i + 1] * V[i + 2]
        return v, F[i] + x + in_plane(v, CY[i], CZ[i])

    def second_sweep(i):
        v, t = total(V1, i)
        V2[i + 1] = (1.0 / 3.0) * v + W[i] * t

    between(second_sweep)
    receive(2, (0, 1))
    both_ends(second_sweep)
    receive(2, (2, 3))
    gains(2)

    def second_rows(i, c):
        at = pl.ds(i, 1)
        V2[i + 1, bottom, :] += jnp.where(low_row, W[i, bottom, :] * ygain[0, at, :], 0.0)
        V2[i + 1, top, :] += jnp.where(high_row, W[i, top, :] * ygain[1, at, :], 0.0)
        return c

    lax.fori_loop(0, nx, second_rows, 0)
    send(3, (0, 1))
    pack(3)
    send(3, (2, 3))

    ACC[...] = jnp.zeros_like(ACC)

    def residual(i):
        v, t = total(V2, i)
        ACC[i // POOL] += t - D[i] * v

    between(residual)

    coarse_receive(0)
    gb = GB[...]
    ex, ey, ez = gb.shape
    clane = lax.broadcasted_iota(jnp.int32, gb.shape, 2)
    kx = edge_face(gb[:-1], gb[1:])
    ky = edge_face(gb, pltpu.roll(gb, ey - 1, 1))
    kz = jnp.where(clane == ez - 1, 0.0, edge_face(gb, pltpu.roll(gb, ez - 1, 2)))
    KX[...] = kx
    KY[...] = ky
    KZ[...] = kz
    ends = jnp.where((clane == 0) | (clane == ez - 1), gb, 0.0)
    d = (kz + pltpu.roll(kz, 1, 2)) + (ky + pltpu.roll(ky, 1, 1)) + ends
    d = d[1:-1] + (kx[:-1] + kx[1:])
    KW[pl.ds(1, ex - 2)] = jnp.where(gb[1:-1] > 0, inverse(d), 0.0)

    receive(3, (0, 1))
    both_ends(residual)
    receive(3, (2, 3))
    gains(3)

    def residual_rows(i, c):
        at, g = pl.ds(i, 1), i // POOL
        ACC[g, bottom, :] += jnp.where(low_row, ygain[0, at, :], 0.0)
        ACC[g, top, :] += jnp.where(high_row, ygain[1, at, :], 0.0)
        return c

    lax.fori_loop(0, nx, residual_rows, 0)
    GR[center] = pool(ACC[...]).reshape(cx, cy, cz)
    coarse_send(1)
    coarse_receive(1)

    start, steps = chebyshev_factors()
    lo, hi = 1, ex - 1
    q = GR[pl.ds(lo, hi - lo)] * KW[pl.ds(lo, hi - lo)] * 16.0
    d = q * start
    DD[pl.ds(lo, hi - lo)] = d
    e = DD[center]
    for decay, gain in steps:
        lo, hi = lo + 1, hi - 1
        span = pl.ds(lo, hi - lo)
        v = DD[span]
        ky, kz = KY[span], KZ[span]
        s = KX[pl.ds(lo - 1, hi - lo)] * DD[pl.ds(lo - 1, hi - lo)]
        s = s + KX[span] * DD[pl.ds(lo + 1, hi - lo)]
        s = s + (ky * pltpu.roll(v, ey - 1, 1) + pltpu.roll(ky * v, 1, 1))
        s = s + (kz * pltpu.roll(v, ez - 1, 2) + pltpu.roll(kz * v, 1, 2))
        q = q[1:-1] - v + KW[span] * s
        DD[span] = decay * v + gain * q
        e = e + DD[center]
    ACC[...] = expand(e.reshape(cx * cy, cz), cx * ny).reshape(cx, ny, nz)
    stores = []
    for g in range(cx):
        tall = ACC[g]
        for k in range(POOL * g, POOL * (g + 1)):
            T[k] = V2[k + 1] + tall
        planes = pl.ds(POOL * g, POOL)
        stores.append(pltpu.make_async_copy(T.at[planes], out_hbm.at[planes], lsem.at[3 + g]))
        stores[-1].start()

    for a in range(4):
        for way in range(4):
            @pl.when(there(*goes[way]))
            def _():
                fine_copy(a, way).wait_send()
    for a in range(2):
        for o, (dx, dg) in enumerate(offsets):
            @pl.when(there(dx, dg))
            def _():
                coarse_copy(a, o).wait_send()
    for store in stores:
        store.wait()


def per_device(nb, ng, right_side, inv_density, pressure):
    nx, ny, nz = right_side.shape
    cx, cy, cz = nx // POOL, ny // POOL, nz // POOL
    hb, hg = -(-CHEB // cx), -(-CHEB // cy)
    ex, ey = (2 * hb + 1) * cx, (2 * hg + 1) * cy
    count = (2 * hb + 1) * (2 * hg + 1) - 1
    f32 = jnp.float32
    block = pltpu.VMEM((nx, ny, nz), f32)
    padded = pltpu.VMEM((nx + 2, ny, nz), f32)
    coarse = pltpu.VMEM((ex, ey, cz), f32)
    dma = pltpu.SemaphoreType.DMA
    hbm = pl.BlockSpec(memory_space=pltpu.HBM)
    return pl.pallas_call(
        functools.partial(cycle_kernel, nb, ng),
        out_shape=jax.ShapeDtypeStruct((nx, ny, nz), f32),
        in_specs=[hbm] * 3,
        out_specs=pl.BlockSpec(memory_space=pl.ANY),
        scratch_shapes=[
            padded, padded, padded, padded,
            block,
            pltpu.VMEM((nx + 1, ny, nz), f32),
            block, block, block, block, block,
            pltpu.VMEM((4, 2, nx, nz), f32),
            pltpu.VMEM((4, 2, nx, nz), f32),
            pltpu.VMEM((2, nx, nz), f32),
            pltpu.VMEM((2, nx, nz), f32),
            pltpu.VMEM((cx, ny, nz), f32),
            coarse, coarse,
            pltpu.VMEM((ex - 1, ey, cz), f32),
            coarse, coarse, coarse, coarse,
            dma((3 + cx,)), dma((4, 4)), dma((4, 4)), dma((2, count)), dma((2, count)),
        ],
        compiler_params=pltpu.CompilerParams(
            collective_id=0, has_side_effects=True, vmem_limit_bytes=52 * 1024 * 1024
        ),
        name="cycle",
    )(right_side, inv_density, pressure)


def solution(mesh):
    spec = P("box", "group", None)
    return jax.shard_map(
        functools.partial(per_device, mesh.shape["box"], mesh.shape["group"]),
        mesh=mesh,
        in_specs=(spec, spec, spec),
        out_specs=spec,
        check_vma=False,
    )
```
